256 devices in a mesh: lat: 16 (over y_lo, x, core), lon: 16 (over z, y_hi).
Axes of the slice: x: 4, y: 4 (y_hi: 2, y_lo: 2; y = y_hi * 2 + y_lo), z: 8, core: 2. Of those that a mesh axis runs over, the one named last changes fastest.
Arguments:
- nodes: bfloat16 [64, 32, 128, 512], P('lat', 'lon'), may hold values from -6 to 6
- neighbours: int32 [64, 32, 12], P('lat', 'lon'), may hold values from 0 to 2047, as said below
- live: int32 [64, 32], P('lat', 'lon'), may hold values from 6 to 12
- gain_attn: float32 [512], replicated, may hold values from 0.25 to 1.75
- w_query: bfloat16 [512, 512], replicated, may hold values from -2 to 2
- w_key: bfloat16 [512, 512], replicated, may hold values from -2 to 2
- w_value: bfloat16 [512, 512], replicated, may hold values from -0.25 to 0.25
- w_out: bfloat16 [512, 512], replicated, may hold values from -0.25 to 0.25
- gain_mlp: float32 [512], replicated, may hold values from 0.25 to 1.75
- w_in: bfloat16 [512, 2048], replicated, may hold values from -0.25 to 0.25
- w_back: bfloat16 [2048, 512], replicated, may hold values from -0.125 to 0.125
Outputs:
- updated: bfloat16 [64, 32, 128, 512], P('lat', 'lon')
The draws below stay inside these ranges and needn't reach their ends.
Inputs may be any that keep to these rules, and one draw needn't show every extreme that they name: `neighbours`: slot 0 of each block is the block itself; slots below live name distinct blocks; every named block lies at most 1 block row and at most 2 block columns away, columns counted around the sphere modulo 32, and inside rows 0 to 63.
All inputs are finite; a program needn't handle non-finite values.
Results may differ from the reference program's by a relative error of at most 0.006.
Values may be sent and summed in bfloat16 or wider, within the bound.
No kernel may reach another device: no remote copies, remote signals or barrier semaphores. Data moves between devices by JAX's collectives and lax.ppermute only.
A program may use at most 128 MiB of HBM per device.

```python
import jax
import jax.numpy as jnp
from jax import lax

D = 512
HEADS = 8
FFN = 2048
NODE_BLK = 128
NBR = 12
NBL = 64
NBO = 32


def neighbour_table(key):
    key = jax.random.fold_in(key, 5)
    lat = jnp.arange(NBL, dtype=jnp.int32)[:, None, None]
    lon = jnp.arange(NBO, dtype=jnp.int32)[None, :, None]
    cand = jnp.arange(15, dtype=jnp.int32)
    dlat = cand // 5 - 1
    dlon = cand % 5 - 2
    target = lat + dlat[None, None, :]
    valid = (target >= 0) & (target < NBL)
    valid = jnp.broadcast_to(valid, (NBL, NBO, 15))
    noise = jax.random.randint(key, (NBL, NBO, 15), 0, 1 << 20)
    score = noise * 16 + cand
    score = jnp.where(cand == 7, -1, score)
    score = jnp.where(valid, score, (1 << 25) + cand)
    order = jnp.argsort(score, axis=-1, stable=True)[:, :, :NBR]
    pick_lat = jnp.take_along_axis(jnp.broadcast_to(target, (NBL, NBO, 15)), order, axis=-1)
    pick_lon = (lon + dlon[order]) % NBO
    pick_ok = jnp.take_along_axis(valid, order, axis=-1)
    selfid = lat * NBO + lon
    ids = jnp.where(pick_ok, pick_lat * NBO + pick_lon, selfid)
    nvalid = jnp.minimum(jnp.sum(valid.astype(jnp.int32), axis=-1), NBR)
    return (ids.astype(jnp.int32), nvalid.astype(jnp.int32))


def draw_neighbours(key, part):
    ids, nvalid = neighbour_table(key)
    return ids


def draw_live(key, part):
    ids, nvalid = neighbour_table(key)
    key = jax.random.fold_in(key, 11)
    count = jax.random.randint(key, (NBL, NBO), 6, NBR + 1)
    count = jnp.minimum(count, nvalid)
    lon = jnp.arange(NBO, dtype=jnp.int32)[None, :]
    count = jnp.where(lon == 0, nvalid, count)
    return count.astype(jnp.int32)


def draw_w_query(key, part):
    key = jax.random.fold_in(key, 1)
    result = jnp.clip(jax.random.normal(key, (D, D), jnp.float32), -6.0, 6.0) / D ** 0.5
    return jnp.clip(result, -2.0, 2.0).astype(jnp.bfloat16)


def draw_w_key(key, part):
    key = jax.random.fold_in(key, 2)
    other = jnp.clip(jax.random.normal(key, (D, D), jnp.float32), -6.0, 6.0)
    result = other / D ** 0.5
    return jnp.clip(result, -2.0, 2.0).astype(jnp.bfloat16)


def levels(key, dims, split, low, largest):
    factor_of = 1.0
    for axis_at, parts in split:
        draws = jax.random.uniform(jax.random.fold_in(jax.random.fold_in(key, 6), axis_at), (parts,), jnp.float32, low / len(split), largest / len(split))
        factor_of = factor_of * jnp.repeat(jnp.exp(draws), dims[axis_at] // parts).reshape((-1,) + (1,) * (len(dims) - 1 - axis_at))
    return factor_of


def bell_draw(rng, shape, scale, limit, shards=(), kind=jnp.bfloat16):
    values = scale * jax.random.normal(rng, shape, jnp.float32)
    if shards:
        values = values * levels(rng, shape, shards, -0.22, 0.18)
    return jnp.clip(values, -limit, limit).astype(kind)


def setup_inputs(seed: int = 0) -> dict:
    splits = jax.random.split(jax.random.key(seed), 12)
    return {
        "nodes": bell_draw(splits[0], (NBL, NBO, NODE_BLK, D), 1.0, 6.0, ((0, 16), (1, 16))),
        "neighbours": draw_neighbours(jax.random.fold_in(splits[11], 71), 0),
        "live": draw_live(jax.random.fold_in(splits[11], 71), 0),
        "gain_attn": jnp.clip(1.0 + 0.15 * jax.random.normal(splits[3], (D,), jnp.float32), 0.25, 1.75),
        "w_query": draw_w_query(jax.random.fold_in(splits[11], 71), 0),
        "w_key": draw_w_key(jax.random.fold_in(splits[11], 71), 0),
        "w_value": bell_draw(splits[6], (D, D), D ** -0.5, 0.25),
        "w_out": bell_draw(splits[7], (D, D), D ** -0.5, 0.25),
        "gain_mlp": jnp.clip(1.0 + 0.15 * jax.random.normal(splits[8], (D,), jnp.float32), 0.25, 1.75),
        "w_in": bell_draw(splits[9], (D, FFN), D ** -0.5, 0.25),
        "w_back": bell_draw(splits[10], (FFN, D), FFN ** -0.5, 0.125),
    }


def normalize(values, gain):
    centre = values - lax.optimization_barrier(jnp.mean(values, axis=-1, keepdims=True))
    spread = lax.optimization_barrier(jnp.mean(centre * centre, axis=-1, keepdims=True))
    return centre * lax.rsqrt(spread + 1e-05) * gain

def attend(query, gathered, count):
    groups = query.shape[0]
    width = query.shape[-1]
    head_dim = width // HEADS
    nkeys = gathered.shape[1]
    qh = query.astype(jnp.float32).reshape(groups, NODE_BLK, HEADS, head_dim)
    kh = gathered[..., :width].astype(jnp.float32).reshape(groups, nkeys, HEADS, head_dim)
    vh = gathered[..., width:].astype(jnp.float32).reshape(groups, nkeys, HEADS, head_dim)
    scores = jnp.einsum('gqhd,gkhd->ghqk', qh, kh) * (1.0 / head_dim ** 0.5)
    slots = jnp.arange(nkeys, dtype=jnp.int32) // NODE_BLK
    usable = slots[None, :] < count[:, None]
    scores = jnp.where(usable[:, None, None, :], scores, jnp.float32(-1e+30))
    top = lax.optimization_barrier(jnp.max(scores, axis=-1, keepdims=True))
    expo = jnp.exp(scores - top)
    probs = expo / lax.optimization_barrier(jnp.sum(expo, axis=-1, keepdims=True))
    weights = probs.astype(jnp.bfloat16).astype(jnp.float32)
    out = jnp.einsum('ghqk,gkhd->gqhd', weights, vh)
    return out.astype(jnp.bfloat16).reshape(groups, NODE_BLK, width)

def reference(nodes, neighbours, live, gain_attn, w_query, w_key, w_value, w_out, gain_mlp, w_in, w_back):
    rows, cols, nblk, width = nodes.shape
    blocks = rows * cols
    flat = nodes.astype(jnp.float32).reshape(-1, width)
    normed = normalize(flat, gain_attn).astype(jnp.bfloat16)
    query = jnp.dot(normed, w_query, preferred_element_type=jnp.float32).astype(jnp.bfloat16)
    keys = jnp.dot(normed, w_key, preferred_element_type=jnp.float32).astype(jnp.bfloat16)
    values = jnp.dot(normed, w_value, preferred_element_type=jnp.float32).astype(jnp.bfloat16)
    stacked = jnp.concatenate([keys, values], axis=-1).reshape(blocks, nblk, 2 * width)
    group = 8
    ids = neighbours.reshape(blocks // group, group, NBR)
    counts = live.reshape(blocks // group, group)
    qgroups = query.reshape(blocks // group, group, nblk, width)

    def one(args):
        qg, ig, cg = args
        gathered = stacked[ig].reshape(group, NBR * nblk, 2 * width)
        return attend(qg, gathered, cg)
    attended = lax.map(one, (qgroups, ids, counts)).reshape(-1, width)
    mid = flat + jnp.dot(attended, w_out, preferred_element_type=jnp.float32)
    second = normalize(mid, gain_mlp).astype(jnp.bfloat16)
    inner = jax.nn.gelu(jnp.dot(second, w_in, preferred_element_type=jnp.float32), approximate=True).astype(jnp.bfloat16)
    updated = mid + jnp.dot(inner, w_back, preferred_element_type=jnp.float32)
    return updated.astype(jnp.bfloat16).reshape(rows, cols, nblk, width)
```

```python
import math

import jax
import jax.numpy as jnp
from jax import lax
from jax.experimental import pallas as pl
from jax.experimental.pallas import tpu as pltpu
from jax.sharding import PartitionSpec as P

HEADS = 8
NBR = 12
NULL = 36
AXES = ("lat", "lon")
F32 = jnp.float32
BF16 = jnp.bfloat16
NT = (((1,), (1,)), ((), ()))


def moved(value, target):
    lats, lons = lax.axis_size("lat"), lax.axis_size("lon")
    pairs = []
    for la in range(lats):
        for lo in range(lons):
            to = target(la, lo)
            if to is not None:
                pairs.append((la * lons + lo, to[0] * lons + to[1]))
    return lax.ppermute(value, AXES, pairs)


def to_partner(value):
    return moved(value, lambda la, lo: (la, lo ^ 1))


def along_z(value):
    lons = lax.axis_size("lon")
    return moved(value, lambda la, lo: (la, (lo + (2 if lo % 2 == 0 else -2)) % lons))


def to_next_lat(value):
    lats = lax.axis_size("lat")
    return moved(value, lambda la, lo: (la + 1, lo) if la + 1 < lats else None)


def to_last_lat(value):
    return moved(value, lambda la, lo: (la - 1, lo) if la > 0 else None)


def slots_of(neighbours, live, rows, cols):
    total_lon = cols * lax.axis_size("lon")
    lat = lax.axis_index("lat")
    lon = lax.axis_index("lon")
    dr = neighbours // total_lon - lat * rows
    dc = (neighbours % total_lon - lon * cols + 2) % total_lon
    side = jnp.where(dc < 2, 0, 1)
    partner_side = jnp.where(lon % 2 == 0, 1, 0)
    kind = jnp.where((dc == 2) | (dc == 3), 0, jnp.where(side == partner_side, 1, 2))
    col = dc % 2
    place = jnp.where(dr == 0, 0, jnp.where(dr == 3, 1, dr + 1))
    place = jnp.where(kind == 0, dr, place)
    inner = kind * 8 + place * 2 + col
    edge = kind * 2 + col
    slot = jnp.where(dr < 0, 24 + edge, jnp.where(dr >= rows, 30 + edge, inner))
    usable = jnp.arange(NBR, dtype=jnp.int32) < live[..., None]
    slot = jnp.where(usable, jnp.clip(slot, 0, NULL), NULL)
    return slot.reshape(rows * cols, NBR)


def normalize(x, gain):
    centre = x - jnp.mean(x, axis=-1, keepdims=True)
    spread = jnp.mean(centre * centre, axis=-1, keepdims=True)
    return centre * lax.rsqrt(spread + 1e-05) * gain


def dot(a, b):
    return jnp.dot(a, b, preferred_element_type=F32)


def layer_kernel(
    slots, counts,
    own, par_o, par_i, far_o, far_i, up, down,
    gain_attn, wq_t, wk, wv_t, wo, gain_mlp, w_in, w_back,
    out,
    kscr, vscr, qscr, att, chk,
):
    pairs_all = (
        (own, 0, 4), (par_o, 8, 2), (par_i, 12, 2), (far_o, 16, 2), (far_i, 20, 2),
        (up, 24, 3), (down, 30, 3),
    )
    kscr[NULL] = jnp.zeros((128, 512), BF16)
    vscr[NULL] = jnp.zeros((4, 144, 128), BF16)
    chk[...] = jnp.zeros_like(chk)
    zeros = jnp.zeros((64, 128), BF16)

    for src, base, n in pairs_all:
        def project(i, carry, src=src, base=base):
            at = base + 2 * i
            x = src[pl.ds(2 * i, 2)].astype(F32).reshape(256, 512)
            y = normalize(x, gain_attn[...]).astype(BF16)
            k = dot(y, wk[...]).astype(BF16)
            kscr[at] = k[:128]
            kscr[at + 1] = k[128:]
            vt = lax.dot_general(wv_t[...], y, NT, preferred_element_type=F32).astype(BF16)
            for blk in range(2):
                for hp in range(4):
                    vscr[at + blk, hp, pl.ds(0, 128)] = vt[hp * 128:(hp + 1) * 128, blk * 128:(blk + 1) * 128]
                    vscr[at + blk, hp, pl.ds(128, 16)] = jnp.ones((16, 128), BF16)
            if src is own:
                qt = lax.dot_general(wq_t[...], y, NT, preferred_element_type=F32).astype(BF16)
                qt = (qt * 0.125).astype(BF16)
                for blk in range(2):
                    for hp in range(4):
                        h0 = qt[hp * 128:hp * 128 + 64, blk * 128:(blk + 1) * 128]
                        h1 = qt[hp * 128 + 64:(hp + 1) * 128, blk * 128:(blk + 1) * 128]
                        qscr[at + blk, hp, pl.ds(0, 64)] = jnp.concatenate([h0, zeros], axis=1)
                        qscr[at + blk, hp, pl.ds(64, 64)] = jnp.concatenate([zeros, h1], axis=1)
            return carry
        lax.fori_loop(0, n, project, 0)

    def finish(o, den):
        inv = 1.0 / den
        h0 = o[0:64, 0:128] * inv[:, 0:128]
        h1 = o[64:128, 128:256] * inv[:, 128:256]
        return jnp.concatenate([h0, h1], axis=0)

    def attend(b, carry):
        ids = [slots[b, n] for n in range(NBR)]
        parts = []
        bad = jnp.zeros((1, 256), F32)
        for hp in range(4):
            q = qscr[b, hp]
            keys = jnp.concatenate([kscr[i, :, hp * 128:(hp + 1) * 128] for i in ids], axis=0)
            p = jnp.exp(dot(keys, q)).astype(BF16)
            vals = jnp.concatenate([vscr[i, hp] for i in ids], axis=1)
            o = dot(vals, p)
            den = o[128:129]
            good = (den > 2.0 ** -60) & (den < 2.0 ** 100)
            bad = jnp.maximum(bad, jnp.where(good, 0.0, 1.0))
            parts.append(finish(o, den))
        chk[...] = jnp.maximum(chk[...], bad)
        full = jnp.concatenate(parts, axis=0)
        att[pl.ds(pl.multiple_of(b * 128, 128), 128)] = full.T.astype(BF16)
        return carry

    lax.fori_loop(0, 8, attend, 0)

    @pl.when(jnp.max(chk[...]) > 0.5)
    def _():
        def attend_shifted(b, carry):
            parts = []
            for hp in range(4):
                q = qscr[b, hp]

                def scores(n, hp=hp, q=q):
                    return dot(kscr[slots[b, n], :, hp * 128:(hp + 1) * 128], q)

                def top_of(n, m):
                    return jnp.maximum(m, jnp.max(scores(n), axis=0, keepdims=True))

                top = lax.fori_loop(0, counts[b], top_of, jnp.full((1, 256), -3e38, F32))

                def add(n, o, hp=hp, top=top):
                    p = jnp.exp(scores(n) - top).astype(BF16)
                    return o + dot(vscr[slots[b, n], hp], p)

                o = lax.fori_loop(0, counts[b], add, jnp.zeros((144, 256), F32))
                parts.append(finish(o, o[128:129]))
            full = jnp.concatenate(parts, axis=0)
            att[pl.ds(pl.multiple_of(b * 128, 128), 128)] = full.T.astype(BF16)
            return carry

        lax.fori_loop(0, 8, attend_shifted, 0)

    def mlp(i, carry):
        x = own[pl.ds(2 * i, 2)].astype(F32).reshape(256, 512)
        a = att[pl.ds(pl.multiple_of(i * 256, 256), 256)]
        mid = x + dot(a, wo[...])
        y = normalize(mid, gain_mlp[...]).astype(BF16)
        inner = jax.nn.gelu(dot(y, w_in[...]), approximate=True).astype(BF16)
        res = mid + dot(inner, w_back[...])
        out[pl.ds(2 * i, 2)] = res.astype(BF16).reshape(2, 128, 512)
        return carry

    lax.fori_loop(0, 4, mlp, 0)


def shards(
    nodes, neighbours, live, gain_attn, w_query, w_key, w_value, w_out, gain_mlp, w_in, w_back
):
    rows, cols, nblk, width = nodes.shape
    blocks = rows * cols
    outer = jnp.concatenate([nodes[:1], nodes[3:]], axis=0)
    par_o = to_partner(outer)
    par_i = to_partner(nodes[1:3])
    far_o = along_z(par_o)
    far_i = along_z(par_i)
    down_row = jnp.concatenate([nodes[3], par_o[1], far_o[1]], axis=0)
    up_row = jnp.concatenate([nodes[0], par_o[0], far_o[0]], axis=0)
    up = to_next_lat(down_row)
    down = to_last_lat(up_row)
    slots = slots_of(neighbours, live, rows, cols)
    flat = lambda v: v.reshape(-1, nblk, width)
    smem = pl.BlockSpec(memory_space=pltpu.SMEM)
    vmem = pl.BlockSpec(memory_space=pltpu.VMEM)
    result = pl.pallas_call(
        layer_kernel,
        out_shape=jax.ShapeDtypeStruct((blocks, nblk, width), BF16),
        in_specs=[smem, smem] + [vmem] * 15,
        out_specs=vmem,
        scratch_shapes=[
            pltpu.VMEM((NULL + 1, 128, 512), BF16),
            pltpu.VMEM((NULL + 1, 4, 144, 128), BF16),
            pltpu.VMEM((8, 4, 128, 256), BF16),
            pltpu.VMEM((1024, 512), BF16),
            pltpu.VMEM((1, 256), F32),
        ],
        compiler_params=pltpu.CompilerParams(vmem_limit_bytes=56 * 2**20),
    )(
        slots, live.reshape(blocks),
        flat(nodes), flat(par_o), flat(par_i), flat(far_o), flat(far_i), up, down,
        gain_attn.reshape(1, width), w_query.T, w_key, w_value.T, w_out, gain_mlp.reshape(1, width), w_in, w_back,
    )
    return result.reshape(rows, cols, nblk, width)


def solution(mesh):
    placed = (
        P("lat", "lon", None, None),
        P("lat", "lon", None),
        P("lat", "lon"),
        P(), P(), P(), P(), P(), P(), P(), P(),
    )
    return jax.shard_map(
        shards, mesh=mesh, in_specs=placed, out_specs=P("lat", "lon", None, None), check_vma=False
    )
```

```python
import jax
import jax.numpy as jnp
from jax import lax
from jax.experimental import pallas as pl
from jax.experimental.pallas import tpu as pltpu
from jax.sharding import PartitionSpec as P

HEADS = 8
NBR = 12
BLK = 128
D = 512
FFN = 2048
PAIRS = 4
AXES = ("lat", "lon")
F32 = jnp.float32
BF16 = jnp.bfloat16
NT = (((1,), (1,)), ((), ()))
FAR_I, UP, DOWN, NULL, OWN, PAR_O, PAR_I, FAR_O, SLOTS = 0, 4, 10, 16, 17, 25, 29, 33, 37
PARTS = ((OWN, PAR_O), (PAR_O, PAR_I), (PAR_I, SLOTS), (FAR_I, NULL))
LENGTHS = {
    (False, 0): (6, 2, 4, 4),
    (False, 1): (6, 2, 6, 2),
    (True, 0): (4, 2, 4, 8),
    (True, 1): (4, 2, 4, 6),
}


def moved(value, target):
    lats, lons = lax.axis_size("lat"), lax.axis_size("lon")
    pairs = []
    for la in range(lats):
        for lo in range(lons):
            to = target(la, lo)
            if to is not None:
                pairs.append((la * lons + lo, to[0] * lons + to[1]))
    return lax.ppermute(value, AXES, pairs)


def to_partner(value):
    return moved(value, lambda la, lo: (la, lo ^ 1))


def along_z(value):
    lons = lax.axis_size("lon")
    return moved(value, lambda la, lo: (la, (lo + (2 if lo % 2 == 0 else -2)) % lons))


def to_next_lat(value):
    lats = lax.axis_size("lat")
    return moved(value, lambda la, lo: (la + 1, lo) if la + 1 < lats else None)


def to_last_lat(value):
    return moved(value, lambda la, lo: (la - 1, lo) if la > 0 else None)


def slots_of(neighbours, live, rows, cols):
    total_lon = cols * lax.axis_size("lon")
    lat = lax.axis_index("lat")
    lon = lax.axis_index("lon")
    dr = neighbours // total_lon - lat * rows
    dc = (neighbours % total_lon - lon * cols + 2) % total_lon
    side = jnp.where(dc < 2, 0, 1)
    partner_side = jnp.where(lon % 2 == 0, 1, 0)
    kind = jnp.where((dc == 2) | (dc == 3), 0, jnp.where(side == partner_side, 1, 2))
    col = dc % 2
    outer = (dr == 0) | (dr == 3)
    place = jnp.where(outer, dr // 3, dr - 1) * 2 + col
    partner = jnp.where(outer, PAR_O, PAR_I) + place
    far = jnp.where(outer, FAR_O, FAR_I) + place
    inner = jnp.where(kind == 0, OWN + dr * 2 + col, jnp.where(kind == 1, partner, far))
    edge = kind * 2 + col
    slot = jnp.where(dr < 0, UP + edge, jnp.where(dr >= rows, DOWN + edge, inner))
    usable = jnp.arange(NBR, dtype=jnp.int32) < live[..., None]
    slot = jnp.where(usable, jnp.clip(slot, 0, SLOTS - 1), NULL)
    return slot.reshape(rows * cols, NBR)


def picked(slots, part):
    low, high = PARTS[part]
    width = max(n[part] for n in LENGTHS.values())
    inside = (slots >= low) & (slots < high)
    place = jnp.cumsum(inside.astype(jnp.int32), axis=-1) - 1
    spot = jnp.where(inside, place, -1)[:, :, None] == jnp.arange(width, dtype=jnp.int32)
    return (high - low) + jnp.sum(jnp.where(spot, slots[:, :, None] - high, 0), axis=1)


def normalize(x, gain):
    centre = x - jnp.mean(x, axis=-1, keepdims=True)
    spread = jnp.mean(centre * centre, axis=-1, keepdims=True)
    return centre * lax.rsqrt(spread + 1e-05) * gain


def dot(a, b):
    return jnp.dot(a, b, preferred_element_type=F32)


def gelu(x):
    half = 0.5 * x
    return half + half * jnp.tanh(x * (0.7978845608028654 + 0.035677408136300125 * (x * x)))


def project(x, gain, wk, wv_t, kscr, vscr, base):
    count = x.shape[0]
    y = normalize(x.astype(F32).reshape(count * BLK, D), gain).astype(BF16)
    k = dot(y, wk).astype(BF16)
    vt = lax.dot_general(wv_t, y, NT, preferred_element_type=F32).astype(BF16)
    for i in range(count):
        kscr[base + i] = k[i * BLK:(i + 1) * BLK]
        for hp in range(PAIRS):
            vscr[base + i, hp, pl.ds(0, BLK)] = vt[hp * BLK:(hp + 1) * BLK, i * BLK:(i + 1) * BLK]
            vscr[base + i, hp, pl.ds(BLK, 16)] = jnp.ones((16, BLK), BF16)
    return y


def clear(kscr, vscr, at):
    kscr[at] = jnp.zeros((BLK, D), BF16)
    vscr[at] = jnp.zeros((PAIRS, 144, BLK), BF16)


def query_of(q, b, hp):
    zeros = jnp.zeros((64, BLK), BF16)
    h0 = q[b, pl.ds(hp * BLK, 64)]
    h1 = q[b, pl.ds(hp * BLK + 64, 64)]
    return jnp.concatenate(
        [jnp.concatenate([h0, zeros], axis=1), jnp.concatenate([zeros, h1], axis=1)], axis=0
    )


def attend(items, q, kscr, vscr, emit):
    work = [(b, hp, ids) for b, ids in items for hp in range(PAIRS)]
    before = None
    for item in work + [None]:
        probs = None
        if item is not None:
            b, hp, ids = item
            qb = query_of(q, b, hp)
            probs = [
                jnp.exp(dot(kscr[i, :, hp * BLK:(hp + 1) * BLK], qb)).astype(BF16) for i in ids
            ]
        if before is not None:
            (b0, hp0, ids0), probs0 = before
            vals = jnp.concatenate([vscr[i, hp0] for i in ids0], axis=1)
            o = dot(vals, jnp.concatenate(probs0, axis=0))
            top = jnp.concatenate([o[0:64, 0:BLK], o[64:BLK, BLK:2 * BLK]], axis=1)
            emit(b0, hp0, top, o[BLK:BLK + 8])
        before = (item, probs)


def blocks_of(parity, edge, side):
    col = jnp.bitwise_xor(parity, side)
    return [r * 2 + col for r in ((0, 3) if edge else (1, 2))]


def attend_part(part, lists, parity, q, kscr, vscr, emit, done):
    for edge in (False, True):
        for side in (0, 1):
            blocks = blocks_of(parity, edge, side)
            n = LENGTHS[(edge, side)][part]
            attend([(b, [lists[b, t] for t in range(n)]) for b in blocks], q, kscr, vscr, emit)
            done(blocks)


class Outgoing:
    def __init__(self, src, dst, sems):
        self.src, self.dst, self.sems, self.copies = src, dst, sems, []

    def send(self, blocks):
        for b in blocks:
            copy = pltpu.make_async_copy(
                self.src.at[b], self.dst.at[b], self.sems.at[len(self.copies)]
            )
            copy.start()
            self.copies.append(copy)

    def wait(self):
        for copy in self.copies:
            copy.wait()


def own_kernel(
    parity, lists, own, gain, wq, wk, wv, q_hbm, state_hbm, wv_t_hbm,
    q, wq_t, wv_t, kscr, vscr, state, sems, in_sems,
):
    clear(kscr, vscr, 8)
    wq_t[...] = wq[...].T
    wv_t[...] = wv[...].T
    w_copy = pltpu.make_async_copy(wv_t, wv_t_hbm, in_sems.at[1])
    w_copy.start()
    for i in range(2):
        y = project(own[pl.ds(4 * i, 4)], gain[...], wk[...], wv_t[...], kscr, vscr, 4 * i)
        qt = lax.dot_general(wq_t[...], y, NT, preferred_element_type=F32).astype(BF16)
        qt = qt * jnp.asarray(0.125, BF16)
        for j in range(4):
            q[4 * i + j] = qt[:, j * BLK:(j + 1) * BLK]
    q_copy = pltpu.make_async_copy(q, q_hbm, in_sems.at[0])
    q_copy.start()
    out = Outgoing(state, state_hbm, sems)

    def emit(b, hp, top, den):
        state[b, hp, pl.ds(0, 64)] = top
        state[b, hp, pl.ds(64, 8)] = den

    attend_part(0, lists, parity[0], q, kscr, vscr, emit, out.send)
    out.wait()
    q_copy.wait()
    w_copy.wait()


def middle_kernel(
    part, parity, lists, *refs
):
    *srcs, gain, wk, wv_t, q_hbm, state_hbm, out_hbm, q, state, kscr, vscr, sems, in_sems = refs
    q_copy = pltpu.make_async_copy(q_hbm, q, in_sems.at[0])
    state_copy = pltpu.make_async_copy(state_hbm, state, in_sems.at[1])
    q_copy.start()
    state_copy.start()
    clear(kscr, vscr, 4 * len(srcs))
    for i, src in enumerate(srcs):
        project(src[...], gain[...], wk[...], wv_t[...], kscr, vscr, 4 * i)
    q_copy.wait()
    state_copy.wait()
    out = Outgoing(state, out_hbm, sems)

    def emit(b, hp, top, den):
        state[b, hp, pl.ds(0, 64)] += top
        state[b, hp, pl.ds(64, 8)] += den

    attend_part(part, lists, parity[0], q, kscr, vscr, emit, out.send)
    out.wait()


def last_kernel(
    parity, lists, slots, counts, far_i, up, down,
    gain_attn, wk, wv_t, gain_mlp, own_hbm, par_o, par_i, far_o, q_hbm, state_hbm, wo_hbm, w_in_hbm, w_back_hbm,
    out_hbm,
    kscr, vscr, att, hid, chk, own, q, state, wo, w_in, w_back, out, sems, out_sems,
):
    late = [
        pltpu.make_async_copy(src, dst, sems.at[i])
        for i, (src, dst) in enumerate(
            (
                (q_hbm, q), (state_hbm, state), (own_hbm, own),
                (wo_hbm, wo), (w_in_hbm, w_in), (w_back_hbm, w_back),
            )
        )
    ]
    for copy in late:
        copy.start()
    clear(kscr, vscr, NULL)
    chk[...] = jnp.zeros_like(chk)
    weights = (gain_attn[...], wk[...], wv_t[...], kscr, vscr)
    project(up[...], *weights, UP)
    project(down[...], *weights, DOWN)
    project(far_i[...], *weights, FAR_I)
    late[0].wait()
    late[1].wait()

    def settle(b, hp, top, den):
        inv = 1.0 / den
        h0 = top[:, 0:BLK] * inv[:, 0:BLK]
        h1 = top[:, BLK:2 * BLK] * inv[:, BLK:2 * BLK]
        both = jnp.concatenate([h0, h1], axis=0).T.astype(BF16)
        att[pl.ds(pl.multiple_of(b * BLK, BLK), BLK), hp * BLK:(hp + 1) * BLK] = both

    def emit(b, hp, top, den):
        top = top + state[b, hp, pl.ds(0, 64)]
        den = den[0:1] + state[b, hp, pl.ds(64, 1)]
        good = (den > 2.0 ** -60) & (den < 2.0 ** 100)
        chk[...] = jnp.maximum(chk[...], jnp.where(good, 0.0, 1.0))
        settle(b, hp, top, den)

    attend_part(3, lists, parity[0], q, kscr, vscr, emit, lambda blocks: None)
    late[2].wait()

    @pl.when(jnp.max(chk[...]) > 0.5)
    def _():
        project(own[pl.ds(0, 4)], *weights, OWN)
        project(own[pl.ds(4, 4)], *weights, OWN + 4)
        for src, base in ((par_o, PAR_O), (par_i, PAR_I), (far_o, FAR_O)):
            copy = pltpu.make_async_copy(src, out.at[pl.ds(0, 4)], sems.at[6])
            copy.start()
            copy.wait()
            project(out[pl.ds(0, 4)], *weights, base)

        def again(b, carry):
            for hp in range(PAIRS):
                qb = query_of(q, b, hp)

                def scores(n, hp=hp, qb=qb):
                    return dot(kscr[slots[b, n], :, hp * BLK:(hp + 1) * BLK], qb)

                def top_of(n, m):
                    return jnp.maximum(m, jnp.max(scores(n), axis=0, keepdims=True))

                top = lax.fori_loop(0, counts[b], top_of, jnp.full((1, 256), -3e38, F32))

                def add(n, o, hp=hp, top=top):
                    p = jnp.exp(scores(n) - top).astype(BF16)
                    return o + dot(vscr[slots[b, n], hp], p)

                o = lax.fori_loop(0, counts[b], add, jnp.zeros((144, 256), F32))
                parts = jnp.concatenate([o[0:64, 0:BLK], o[64:BLK, BLK:2 * BLK]], axis=1)
                settle(b, hp, parts, o[BLK:BLK + 1])
            return carry

        lax.fori_loop(0, 8, again, 0)

    for copy in late[3:]:
        copy.wait()

    sent = []
    for i in range(2):
        mid = own[pl.ds(4 * i, 4)].astype(F32).reshape(512, D) + dot(att[pl.ds(512 * i, 512)], wo[...])
        y = normalize(mid, gain_mlp[...]).astype(BF16)
        for j in range(0, FFN, 256):
            for r in range(0, 512, BLK):
                hid[r:r + BLK, j:j + 256] = gelu(dot(y[r:r + BLK], w_in[:, j:j + 256])).astype(BF16)
        for n in range(0, D, 256):
            res = mid[:, n:n + 256] + dot(hid[...], w_back[:, n:n + 256])
            out[pl.ds(4 * i, 4), :, n:n + 256] = res.astype(BF16).reshape(4, BLK, 256)
        copy = pltpu.make_async_copy(
            out.at[pl.ds(4 * i, 4)], out_hbm.at[pl.ds(4 * i, 4)], out_sems.at[i]
        )
        copy.start()
        sent.append(copy)
    for copy in sent:
        copy.wait()


def shards(
    nodes, neighbours, live, gain_attn, w_query, w_key, w_value, w_out, gain_mlp, w_in, w_back
):
    rows, cols, nblk, width = nodes.shape
    blocks = rows * cols
    smem = pl.BlockSpec(memory_space=pltpu.SMEM)
    vmem = pl.BlockSpec(memory_space=pltpu.VMEM)
    hbm = pl.BlockSpec(memory_space=pltpu.HBM)
    state_shape = (blocks, PAIRS, 72, 256)
    q_shape = (blocks, width, nblk)
    dma = pltpu.SemaphoreType.DMA

    def kv_scratch(count):
        return [
            pltpu.VMEM((count, nblk, width), BF16),
            pltpu.VMEM((count, PAIRS, 144, nblk), BF16),
        ]

    def call(kernel, name, ins, outs, scratch, mib, gflop, mbytes):
        return pl.pallas_call(
            kernel,
            name=name,
            out_shape=[jax.ShapeDtypeStruct(s, t) for s, t in outs],
            in_specs=[i for i, _ in ins],
            out_specs=[hbm] * len(outs),
            scratch_shapes=scratch,
            compiler_params=pltpu.CompilerParams(vmem_limit_bytes=mib * 2**20),
            cost_estimate=pl.CostEstimate(
                flops=int(gflop * 1e9), bytes_accessed=int(mbytes * 1e6), transcendentals=0
            ),
        )(*[v for _, v in ins])

    parity = (lax.axis_index("lon") % 2).astype(jnp.int32).reshape(1)
    slots = slots_of(neighbours, live, rows, cols)
    gain1, gain2 = gain_attn.reshape(1, width), gain_mlp.reshape(1, width)

    own = nodes.reshape(blocks, nblk, width)
    par_o = to_partner(nodes[::3].reshape(4, nblk, width))
    par_i = to_partner(own[2:6])

    q, state, wv_t = call(
        own_kernel, "own_part",
        [(smem, parity), (smem, picked(slots, 0)), (vmem, own), (vmem, gain1)]
        + [(vmem, w_query), (vmem, w_key), (vmem, w_value)],
        [(q_shape, BF16), (state_shape, F32), ((width, width), BF16)],
        [pltpu.VMEM(q_shape, BF16)] + [pltpu.VMEM((width, width), BF16)] * 2 + kv_scratch(9)
        + [pltpu.VMEM(state_shape, F32), dma((8,)), dma((2,))],
        26, 7, 6,
    )
    state, slots, par_o = lax.optimization_barrier((state, slots, par_o))
    lists = [picked(slots, part) for part in range(4)]
    far_o = along_z(par_o)

    def middle(part, name, srcs, state, gflop):
        return call(
            lambda *refs: middle_kernel(part, *refs), name,
            [(smem, parity), (smem, lists[part])] + [(vmem, s) for s in srcs]
            + [(vmem, gain1), (vmem, w_key), (vmem, wv_t), (hbm, q), (hbm, state)],
            [(state_shape, F32)],
            [pltpu.VMEM(q_shape, BF16), pltpu.VMEM(state_shape, F32)] + kv_scratch(4 * len(srcs) + 1)
            + [dma((8,)), dma((2,))],
            26, gflop, 8,
        )[0]

    state = middle(1, "outer_partner_part", [par_o], state, 3)
    state, par_i = lax.optimization_barrier((state, par_i))
    far_i = along_z(par_i)
    far_o, par_i = lax.optimization_barrier((far_o, par_i))
    up_row = jnp.concatenate([own[6:], par_o[2:], far_o[2:]], axis=0)
    down_row = jnp.concatenate([own[:2], par_o[:2], far_o[:2]], axis=0)
    state, up_row, down_row = lax.optimization_barrier((state, up_row, down_row))
    up = to_next_lat(up_row)
    down = to_last_lat(down_row)
    state = middle(2, "inner_partner_part", [par_i, far_o], state, 6)
    (result,) = call(
        last_kernel, "last_part_and_mlp",
        [(smem, parity), (smem, lists[3]), (smem, slots), (smem, live.reshape(blocks))]
        + [(vmem, far_i), (vmem, up), (vmem, down)]
        + [(vmem, gain1), (vmem, w_key), (vmem, wv_t), (vmem, gain2), (hbm, own)]
        + [(hbm, par_o), (hbm, par_i), (hbm, far_o)]
        + [(hbm, q), (hbm, state), (hbm, w_out), (hbm, w_in), (hbm, w_back)],
        [((blocks, nblk, width), BF16)],
        kv_scratch(SLOTS) + [
            pltpu.VMEM((blocks * nblk, width), BF16),
            pltpu.VMEM((512, FFN), BF16),
            pltpu.VMEM((1, 256), F32),
            pltpu.VMEM((blocks, nblk, width), BF16),
            pltpu.VMEM(q_shape, BF16),
            pltpu.VMEM(state_shape, F32),
            pltpu.VMEM((width, width), BF16),
            pltpu.VMEM((width, FFN), BF16),
            pltpu.VMEM((FFN, width), BF16),
            pltpu.VMEM((blocks, nblk, width), BF16),
            dma((7,)),
            dma((2,)),
        ],
        36, 14, 16,
    )
    return result.reshape(rows, cols, nblk, width)


def solution(mesh):
    placed = (
        P("lat", "lon", None, None),
        P("lat", "lon", None),
        P("lat", "lon"),
        P(), P(), P(), P(), P(), P(), P(), P(),
    )
    return jax.shard_map(
        shards, mesh=mesh, in_specs=placed, out_specs=P("lat", "lon", None, None), check_vma=False
    )
```

```python
import jax
import jax.numpy as jnp
from jax import lax
from jax.experimental import pallas as pl
from jax.experimental.pallas import tpu as pltpu
from jax.sharding import PartitionSpec as P

HEADS = 8
NBR = 12
BLK = 128
D = 512
FFN = 2048
PAIRS = 4
COST = 20
AXES = ("lat", "lon")
F32 = jnp.float32
BF16 = jnp.bfloat16
NT = (((1,), (1,)), ((), ()))
FAR_I, UP, DOWN, NULL, OWN, PAR_O, PAR_I, FAR_O, SLOTS = 0, 4, 10, 16, 17, 25, 29, 33, 37
PARTS = ((OWN, PAR_O), (PAR_O, PAR_I), (PAR_I, SLOTS), (FAR_I, NULL))
LENGTHS = {
    (False, 0): (6, 2, 4, 4),
    (False, 1): (6, 2, 6, 2),
    (True, 0): (4, 2, 4, 8),
    (True, 1): (4, 2, 4, 6),
}


def moved(value, target):
    lats, lons = lax.axis_size("lat"), lax.axis_size("lon")
    pairs = []
    for la in range(lats):
        for lo in range(lons):
            to = target(la, lo)
            if to is not None:
                pairs.append((la * lons + lo, to[0] * lons + to[1]))
    return lax.ppermute(value, AXES, pairs)


def to_partner(value):
    return moved(value, lambda la, lo: (la, lo ^ 1))


def along_z(value):
    lons = lax.axis_size("lon")
    return moved(value, lambda la, lo: (la, (lo + (2 if lo % 2 == 0 else -2)) % lons))


def to_next_lat(value):
    lats = lax.axis_size("lat")
    return moved(value, lambda la, lo: (la + 1, lo) if la + 1 < lats else None)


def to_last_lat(value):
    return moved(value, lambda la, lo: (la - 1, lo) if la > 0 else None)


def slots_of(neighbours, live, rows, cols):
    total_lon = cols * lax.axis_size("lon")
    lat = lax.axis_index("lat")
    lon = lax.axis_index("lon")
    dr = neighbours // total_lon - lat * rows
    dc = (neighbours % total_lon - lon * cols + 2) % total_lon
    side = jnp.where(dc < 2, 0, 1)
    partner_side = jnp.where(lon % 2 == 0, 1, 0)
    kind = jnp.where((dc == 2) | (dc == 3), 0, jnp.where(side == partner_side, 1, 2))
    col = dc % 2
    outer = (dr == 0) | (dr == 3)
    place = jnp.where(outer, dr // 3, dr - 1) * 2 + col
    partner = jnp.where(outer, PAR_O, PAR_I) + place
    far = jnp.where(outer, FAR_O, FAR_I) + place
    inner = jnp.where(kind == 0, OWN + dr * 2 + col, jnp.where(kind == 1, partner, far))
    edge = kind * 2 + col
    slot = jnp.where(dr < 0, UP + edge, jnp.where(dr >= rows, DOWN + edge, inner))
    usable = jnp.arange(NBR, dtype=jnp.int32) < live[..., None]
    slot = jnp.where(usable, jnp.clip(slot, 0, SLOTS - 1), NULL)
    return slot.reshape(rows * cols, NBR)


def picked(slots, part):
    low, high = PARTS[part]
    width = max(n[part] for n in LENGTHS.values())
    inside = (slots >= low) & (slots < high)
    place = jnp.cumsum(inside.astype(jnp.int32), axis=-1) - 1
    spot = jnp.where(inside, place, -1)[:, :, None] == jnp.arange(width, dtype=jnp.int32)
    return (high - low) + jnp.sum(jnp.where(spot, slots[:, :, None] - high, 0), axis=1)


def normalize(x, gain):
    centre = x - jnp.mean(x, axis=-1, keepdims=True)
    spread = jnp.mean(centre * centre, axis=-1, keepdims=True)
    return centre * lax.rsqrt(spread + 1e-05) * gain


def dot(a, b):
    return jnp.dot(a, b, preferred_element_type=F32)


def gelu(x):
    half = 0.5 * x
    return half + half * jnp.tanh(x * (0.7978845608028654 + 0.035677408136300125 * (x * x)))


def project(x, gain, wk, wv_t, kscr, vscr, base):
    count = x.shape[0]
    y = normalize(x.astype(F32).reshape(count * BLK, D), gain).astype(BF16)
    k = dot(y, wk).astype(BF16)
    vt = lax.dot_general(wv_t, y, NT, preferred_element_type=F32).astype(BF16)
    for i in range(count):
        kscr[base + i] = k[i * BLK:(i + 1) * BLK]
        for hp in range(PAIRS):
            vscr[base + i, hp, pl.ds(0, BLK)] = vt[hp * BLK:(hp + 1) * BLK, i * BLK:(i + 1) * BLK]
            vscr[base + i, hp, pl.ds(BLK, 16)] = jnp.ones((16, BLK), BF16)
    return y


def clear(kscr, vscr, at):
    kscr[at] = jnp.zeros((BLK, D), BF16)
    vscr[at] = jnp.zeros((PAIRS, 144, BLK), BF16)


def query_of(q, b, hp):
    zeros = jnp.zeros((64, BLK), BF16)
    h0 = q[b, pl.ds(hp * BLK, 64)]
    h1 = q[b, pl.ds(hp * BLK + 64, 64)]
    return jnp.concatenate(
        [jnp.concatenate([h0, zeros], axis=1), jnp.concatenate([zeros, h1], axis=1)], axis=0
    )


def attend(items, q, kscr, vscr, emit):
    work = [(b, hp, ids) for b, ids in items for hp in range(PAIRS)]
    before = None
    for item in work + [None]:
        probs = None
        if item is not None:
            b, hp, ids = item
            qb = query_of(q, b, hp)
            probs = [
                jnp.exp(dot(kscr[i, :, hp * BLK:(hp + 1) * BLK], qb)).astype(BF16) for i in ids
            ]
        if before is not None:
            (b0, hp0, ids0), probs0 = before
            vals = jnp.concatenate([vscr[i, hp0] for i in ids0], axis=1)
            o = dot(vals, jnp.concatenate(probs0, axis=0))
            top = jnp.concatenate([o[0:64, 0:BLK], o[64:BLK, BLK:2 * BLK]], axis=1)
            emit(b0, hp0, top, o[BLK:BLK + 8])
        before = (item, probs)


def blocks_of(parity, edge, side):
    col = jnp.bitwise_xor(parity, side)
    return [r * 2 + col for r in ((0, 3) if edge else (1, 2))]


def attend_part(part, lists, parity, q, kscr, vscr, emit, done):
    for edge in (False, True):
        for side in (0, 1):
            blocks = blocks_of(parity, edge, side)
            n = LENGTHS[(edge, side)][part]
            attend([(b, [lists[b, t] for t in range(n)]) for b in blocks], q, kscr, vscr, emit)
            done(blocks)


def own_kernel(
    parity, lists, own, gain, wq, wk, wv, q, state, wv_t,
    wq_t, kscr, vscr,
):
    clear(kscr, vscr, 8)
    wq_t[...] = wq[...].T
    wv_t[...] = wv[...].T
    for i in range(2):
        y = project(own[pl.ds(4 * i, 4)], gain[...], wk[...], wv_t[...], kscr, vscr, 4 * i)
        qt = lax.dot_general(wq_t[...], y, NT, preferred_element_type=F32).astype(BF16)
        qt = qt * jnp.asarray(0.125, BF16)
        for j in range(4):
            q[4 * i + j] = qt[:, j * BLK:(j + 1) * BLK]
    def emit(b, hp, top, den):
        state[b, hp, pl.ds(0, 64)] = top
        state[b, hp, pl.ds(64, 8)] = den

    attend_part(0, lists, parity[0], q, kscr, vscr, emit, lambda blocks: None)


def middle_kernel(part, parity, lists, *refs):
    *srcs, gain, wk, wv_t, q, state_in, state, kscr, vscr = refs
    clear(kscr, vscr, 4 * len(srcs))
    for i, src in enumerate(srcs):
        project(src[...], gain[...], wk[...], wv_t[...], kscr, vscr, 4 * i)

    def emit(b, hp, top, den):
        state[b, hp, pl.ds(0, 64)] = state_in[b, hp, pl.ds(0, 64)] + top
        state[b, hp, pl.ds(64, 8)] = state_in[b, hp, pl.ds(64, 8)] + den

    attend_part(part, lists, parity[0], q, kscr, vscr, emit, lambda blocks: None)


def last_kernel(
    parity, lists, slots, counts, far_i, up, down,
    gain_attn, wk, wv_t, gain_mlp, own_hbm, par_o, par_i, far_o, q_hbm, state_hbm, wo_hbm, w_in_hbm, w_back_hbm,
    out_hbm,
    kscr, vscr, att, hid, chk, own, q, state, wo, w_in, w_back, out, sems, out_sems,
):
    late = [
        pltpu.make_async_copy(src, dst, sems.at[i])
        for i, (src, dst) in enumerate(
            (
                (q_hbm, q), (state_hbm, state), (own_hbm, own),
                (wo_hbm, wo), (w_in_hbm, w_in), (w_back_hbm, w_back),
            )
        )
    ]
    for copy in late:
        copy.start()
    clear(kscr, vscr, NULL)
    chk[...] = jnp.zeros_like(chk)
    weights = (gain_attn[...], wk[...], wv_t[...], kscr, vscr)
    project(up[...], *weights, UP)
    project(down[...], *weights, DOWN)
    project(far_i[...], *weights, FAR_I)
    late[0].wait()
    late[1].wait()

    def settle(b, hp, top, den):
        inv = 1.0 / den
        h0 = top[:, 0:BLK] * inv[:, 0:BLK]
        h1 = top[:, BLK:2 * BLK] * inv[:, BLK:2 * BLK]
        both = jnp.concatenate([h0, h1], axis=0).T.astype(BF16)
        att[pl.ds(pl.multiple_of(b * BLK, BLK), BLK), hp * BLK:(hp + 1) * BLK] = both

    def emit(b, hp, top, den):
        top = top + state[b, hp, pl.ds(0, 64)]
        den = den[0:1] + state[b, hp, pl.ds(64, 1)]
        good = (den > 2.0 ** -60) & (den < 2.0 ** 100)
        chk[...] = jnp.maximum(chk[...], jnp.where(good, 0.0, 1.0))
        settle(b, hp, top, den)

    attend_part(3, lists, parity[0], q, kscr, vscr, emit, lambda blocks: None)
    late[2].wait()

    @pl.when(jnp.max(chk[...]) > 0.5)
    def _():
        project(own[pl.ds(0, 4)], *weights, OWN)
        project(own[pl.ds(4, 4)], *weights, OWN + 4)
        for src, base in ((par_o, PAR_O), (par_i, PAR_I), (far_o, FAR_O)):
            copy = pltpu.make_async_copy(src, out.at[pl.ds(0, 4)], sems.at[6])
            copy.start()
            copy.wait()
            project(out[pl.ds(0, 4)], *weights, base)

        def again(b, carry):
            for hp in range(PAIRS):
                qb = query_of(q, b, hp)

                def scores(n, hp=hp, qb=qb):
                    return dot(kscr[slots[b, n], :, hp * BLK:(hp + 1) * BLK], qb)

                def top_of(n, m):
                    return jnp.maximum(m, jnp.max(scores(n), axis=0, keepdims=True))

                top = lax.fori_loop(0, counts[b], top_of, jnp.full((1, 256), -3e38, F32))

                def add(n, o, hp=hp, top=top):
                    p = jnp.exp(scores(n) - top).astype(BF16)
                    return o + dot(vscr[slots[b, n], hp], p)

                o = lax.fori_loop(0, counts[b], add, jnp.zeros((144, 256), F32))
                parts = jnp.concatenate([o[0:64, 0:BLK], o[64:BLK, BLK:2 * BLK]], axis=1)
                settle(b, hp, parts, o[BLK:BLK + 1])
            return carry

        lax.fori_loop(0, 8, again, 0)

    for copy in late[3:]:
        copy.wait()

    sent = []
    for i in range(2):
        mid = own[pl.ds(4 * i, 4)].astype(F32).reshape(512, D) + dot(att[pl.ds(512 * i, 512)], wo[...])
        y = normalize(mid, gain_mlp[...]).astype(BF16)
        for j in range(0, FFN, 256):
            for r in range(0, 512, BLK):
                hid[r:r + BLK, j:j + 256] = gelu(dot(y[r:r + BLK], w_in[:, j:j + 256])).astype(BF16)
        for n in range(0, D, 256):
            res = mid[:, n:n + 256] + dot(hid[...], w_back[:, n:n + 256])
            out[pl.ds(4 * i, 4), :, n:n + 256] = res.astype(BF16).reshape(4, BLK, 256)
        copy = pltpu.make_async_copy(
            out.at[pl.ds(4 * i, 4)], out_hbm.at[pl.ds(4 * i, 4)], out_sems.at[i]
        )
        copy.start()
        sent.append(copy)
    for copy in sent:
        copy.wait()


def shards(
    nodes, neighbours, live, gain_attn, w_query, w_key, w_value, w_out, gain_mlp, w_in, w_back
):
    rows, cols, nblk, width = nodes.shape
    blocks = rows * cols
    smem = pl.BlockSpec(memory_space=pltpu.SMEM)
    vmem = pl.BlockSpec(memory_space=pltpu.VMEM)
    hbm = pl.BlockSpec(memory_space=pltpu.HBM)
    state_shape = (blocks, PAIRS, 72, 256)
    q_shape = (blocks, width, nblk)
    dma = pltpu.SemaphoreType.DMA

    def kv_scratch(count):
        return [
            pltpu.VMEM((count, nblk, width), BF16),
            pltpu.VMEM((count, PAIRS, 144, nblk), BF16),
        ]

    def call(kernel, name, ins, outs, scratch, mib, gflop, mbytes, place=hbm):
        return pl.pallas_call(
            kernel,
            name=name,
            out_shape=[jax.ShapeDtypeStruct(s, t) for s, t in outs],
            in_specs=[i for i, _ in ins],
            out_specs=[place] * len(outs),
            scratch_shapes=scratch,
            compiler_params=pltpu.CompilerParams(vmem_limit_bytes=mib * 2**20),
            cost_estimate=pl.CostEstimate(
                flops=int(gflop * COST * 1e9), bytes_accessed=int(mbytes * 1e6), transcendentals=0
            ),
        )(*[v for _, v in ins])

    parity = (lax.axis_index("lon") % 2).astype(jnp.int32).reshape(1)
    slots = slots_of(neighbours, live, rows, cols)
    lists = [picked(slots, part) for part in range(4)]
    gain1, gain2 = gain_attn.reshape(1, width), gain_mlp.reshape(1, width)

    own = nodes.reshape(blocks, nblk, width)
    par_o = to_partner(nodes[::3].reshape(4, nblk, width))
    par_i = to_partner(own[2:6])
    far_o = along_z(par_o)
    q, state, wv_t = call(
        own_kernel, "own_part",
        [(smem, parity), (smem, lists[0]), (vmem, own), (vmem, gain1)]
        + [(vmem, w_query), (vmem, w_key), (vmem, w_value)],
        [(q_shape, BF16), (state_shape, F32), ((width, width), BF16)],
        [pltpu.VMEM((width, width), BF16)] + kv_scratch(9),
        26, 7, 6, vmem,
    )

    def middle(part, name, srcs, state, gflop):
        return call(
            lambda *refs: middle_kernel(part, *refs), name,
            [(smem, parity), (smem, lists[part])] + [(vmem, s) for s in srcs]
            + [(vmem, gain1), (vmem, w_key), (vmem, wv_t), (vmem, q), (vmem, state)],
            [(state_shape, F32)],
            kv_scratch(4 * len(srcs) + 1),
            22, gflop, 8, vmem,
        )[0]

    state = middle(1, "outer_partner_part", [par_o], state, 3)
    state, par_i = lax.optimization_barrier((state, par_i))
    far_i = along_z(par_i)
    own_e, par_e, far_e, _ = lax.optimization_barrier((own, par_o, far_o, par_i))
    up = to_next_lat(jnp.concatenate([own_e[6:], par_e[2:], far_e[2:]], axis=0))
    down = to_last_lat(jnp.concatenate([own_e[:2], par_e[:2], far_e[:2]], axis=0))
    state = middle(2, "inner_partner_part", [par_i, far_o], state, 6)
    (result,) = call(
        last_kernel, "last_part_and_mlp",
        [(smem, parity), (smem, lists[3]), (smem, slots), (smem, live.reshape(blocks))]
        + [(vmem, far_i), (vmem, up), (vmem, down)]
        + [(vmem, gain1), (vmem, w_key), (vmem, wv_t), (vmem, gain2), (hbm, own)]
        + [(hbm, par_o), (hbm, par_i), (hbm, far_o)]
        + [(hbm, q), (hbm, state), (hbm, w_out), (hbm, w_in), (hbm, w_back)],
        [((blocks, nblk, width), BF16)],
        kv_scratch(SLOTS) + [
            pltpu.VMEM((blocks * nblk, width), BF16),
            pltpu.VMEM((512, FFN), BF16),
            pltpu.VMEM((1, 256), F32),
            pltpu.VMEM((blocks, nblk, width), BF16),
            pltpu.VMEM(q_shape, BF16),
            pltpu.VMEM(state_shape, F32),
            pltpu.VMEM((width, width), BF16),
            pltpu.VMEM((width, FFN), BF16),
            pltpu.VMEM((FFN, width), BF16),
            pltpu.VMEM((blocks, nblk, width), BF16),
            dma((7,)),
            dma((2,)),
        ],
        36, 14, 16,
    )
    return result.reshape(rows, cols, nblk, width)


def solution(mesh):
    placed = (
        P("lat", "lon", None, None),
        P("lat", "lon", None),
        P("lat", "lon"),
        P(), P(), P(), P(), P(), P(), P(), P(),
    )
    return jax.shard_map(
        shards, mesh=mesh, in_specs=placed, out_specs=P("lat", "lon", None, None), check_vma=False
    )
```

```python
import jax
import jax.numpy as jnp
from jax import lax
from jax.experimental import pallas as pl
from jax.experimental.pallas import tpu as pltpu
from jax.sharding import PartitionSpec as P

HEADS = 8
NBR = 12
BLK = 128
D = 512
FFN = 2048
PAIRS = 4
COST = 20
AXES = ("lat", "lon")
F32 = jnp.float32
BF16 = jnp.bfloat16
NT = (((1,), (1,)), ((), ()))
FAR_I, UP, DOWN, NULL, OWN, PAR_O, PAR_I, FAR_O, SLOTS = 0, 4, 10, 16, 17, 25, 29, 33, 37
PARTS = ((OWN, PAR_O), (PAR_O, PAR_I), (PAR_I, SLOTS), (FAR_I, NULL))
LENGTHS = {
    (False, 0): (6, 2, 4, 4),
    (False, 1): (6, 2, 6, 2),
    (True, 0): (4, 2, 4, 8),
    (True, 1): (4, 2, 4, 6),
}


def moved(value, target):
    lats, lons = lax.axis_size("lat"), lax.axis_size("lon")
    pairs = []
    for la in range(lats):
        for lo in range(lons):
            to = target(la, lo)
            if to is not None:
                pairs.append((la * lons + lo, to[0] * lons + to[1]))
    return lax.ppermute(value, AXES, pairs)


def to_partner(value):
    return moved(value, lambda la, lo: (la, lo ^ 1))


def along_z(value):
    lons = lax.axis_size("lon")
    return moved(value, lambda la, lo: (la, (lo + (2 if lo % 2 == 0 else -2)) % lons))


def to_next_lat(value):
    lats = lax.axis_size("lat")
    return moved(value, lambda la, lo: (la + 1, lo) if la + 1 < lats else None)


def to_last_lat(value):
    return moved(value, lambda la, lo: (la - 1, lo) if la > 0 else None)


def slots_of(neighbours, live, rows, cols):
    total_lon = cols * lax.axis_size("lon")
    lat = lax.axis_index("lat")
    lon = lax.axis_index("lon")
    dr = neighbours // total_lon - lat * rows
    dc = (neighbours % total_lon - lon * cols + 2) % total_lon
    side = jnp.where(dc < 2, 0, 1)
    partner_side = jnp.where(lon % 2 == 0, 1, 0)
    kind = jnp.where((dc == 2) | (dc == 3), 0, jnp.where(side == partner_side, 1, 2))
    col = dc % 2
    outer = (dr == 0) | (dr == 3)
    place = jnp.where(outer, dr // 3, dr - 1) * 2 + col
    partner = jnp.where(outer, PAR_O, PAR_I) + place
    far = jnp.where(outer, FAR_O, FAR_I) + place
    inner = jnp.where(kind == 0, OWN + dr * 2 + col, jnp.where(kind == 1, partner, far))
    edge = kind * 2 + col
    slot = jnp.where(dr < 0, UP + edge, jnp.where(dr >= rows, DOWN + edge, inner))
    usable = jnp.arange(NBR, dtype=jnp.int32) < live[..., None]
    slot = jnp.where(usable, jnp.clip(slot, 0, SLOTS - 1), NULL)
    return slot.reshape(rows * cols, NBR)


def picked(slots, part):
    low, high = PARTS[part]
    width = max(n[part] for n in LENGTHS.values())
    inside = (slots >= low) & (slots < high)
    place = jnp.cumsum(inside.astype(jnp.int32), axis=-1) - 1
    spot = jnp.where(inside, place, -1)[:, :, None] == jnp.arange(width, dtype=jnp.int32)
    return (high - low) + jnp.sum(jnp.where(spot, slots[:, :, None] - high, 0), axis=1)


def normalize(x, gain):
    centre = x - jnp.mean(x, axis=-1, keepdims=True)
    spread = jnp.mean(centre * centre, axis=-1, keepdims=True)
    return centre * lax.rsqrt(spread + 1e-05) * gain


def dot(a, b):
    return jnp.dot(a, b, preferred_element_type=F32)


def gelu(x):
    half = 0.5 * x
    return half + half * jnp.tanh(x * (0.7978845608028654 + 0.035677408136300125 * (x * x)))


def project(x, gain, wk, wv_t, kscr, vscr, base):
    count = x.shape[0]
    y = normalize(x.astype(F32).reshape(count * BLK, D), gain).astype(BF16)
    k = dot(y, wk).astype(BF16)
    vt = lax.dot_general(wv_t, y, NT, preferred_element_type=F32).astype(BF16)
    for i in range(count):
        kscr[base + i] = k[i * BLK:(i + 1) * BLK]
        for hp in range(PAIRS):
            vscr[base + i, hp, pl.ds(0, BLK)] = vt[hp * BLK:(hp + 1) * BLK, i * BLK:(i + 1) * BLK]
            vscr[base + i, hp, pl.ds(BLK, 16)] = jnp.ones((16, BLK), BF16)
    return y


def clear(kscr, vscr, at):
    kscr[at] = jnp.zeros((BLK, D), BF16)
    vscr[at] = jnp.zeros((PAIRS, 144, BLK), BF16)


def head_lanes(hp):
    return pl.ds(hp * BLK if isinstance(hp, int) else pl.multiple_of(hp * BLK, BLK), BLK)


def query_of(q, b, hp):
    zeros = jnp.zeros((64, BLK), BF16)
    h0 = q[b, pl.ds(hp * BLK, 64)]
    h1 = q[b, pl.ds(hp * BLK + 64, 64)]
    return jnp.concatenate(
        [jnp.concatenate([h0, zeros], axis=1), jnp.concatenate([zeros, h1], axis=1)], axis=0
    )


def attend(items, q, kscr, vscr, emit):
    work = [(b, hp, ids) for b, ids in items for hp in range(PAIRS)]
    before = None
    for item in work + [None]:
        probs = None
        if item is not None:
            b, hp, ids = item
            qb = query_of(q, b, hp)
            probs = [
                jnp.exp(dot(kscr[i, :, hp * BLK:(hp + 1) * BLK], qb)).astype(BF16) for i in ids
            ]
        if before is not None:
            (b0, hp0, ids0), probs0 = before
            vals = jnp.concatenate([vscr[i, hp0] for i in ids0], axis=1)
            o = dot(vals, jnp.concatenate(probs0, axis=0))
            top = jnp.concatenate([o[0:64, 0:BLK], o[64:BLK, BLK:2 * BLK]], axis=1)
            emit(b0, hp0, top, o[BLK:BLK + 8])
        before = (item, probs)


def attend_part(part, lists, parity, q, kscr, vscr, emit):
    groups = {}
    for (edge, side), lengths in LENGTHS.items():
        groups.setdefault(lengths[part], []).append((int(edge), side))
    for n, members in groups.items():
        at_once = 1 if part == 2 else 2

        def some(j, carry, n=n, members=members, at_once=at_once):
            items = []
            for e in range(at_once):
                i = j * at_once + e
                member, second = i // 2, i % 2
                edge, side = members[0]
                for m in range(1, len(members)):
                    edge = jnp.where(member == m, members[m][0], edge)
                    side = jnp.where(member == m, members[m][1], side)
                row = edge * 3 * second + (1 - edge) * (1 + second)
                b = row * 2 + jnp.bitwise_xor(parity, side)
                items.append((b, [lists[b, t] for t in range(n)]))
            attend(items, q, kscr, vscr, emit)
            return carry

        lax.fori_loop(0, 2 * len(members) // at_once, some, 0)


def fetch(pairs, sems):
    copies = [pltpu.make_async_copy(src, dst, sems.at[i]) for i, (src, dst) in enumerate(pairs)]
    for copy in copies:
        copy.start()
    return copies


def project_in_place(count, per, gain, wk, wv_t, kscr, vscr, base):
    def some(i, carry):
        at = base + per * i
        project(kscr[pl.ds(at, per)], gain[...], wk[...], wv_t[...], kscr, vscr, at)
        return carry

    lax.fori_loop(0, count // per, some, 0)


def own_kernel(
    parity, lists, own, gain, wq, wk, wv, q, state, wv_t,
    wq_t, kscr, vscr,
):
    clear(kscr, vscr, 8)
    wq_t[...] = wq[...].T
    wv_t[...] = wv[...].T

    def some(i, carry):
        y = project(own[pl.ds(4 * i, 4)], gain[...], wk[...], wv_t[...], kscr, vscr, 4 * i)
        qt = lax.dot_general(wq_t[...], y, NT, preferred_element_type=F32).astype(BF16)
        qt = qt * jnp.asarray(0.125, BF16)
        for j in range(4):
            q[4 * i + j] = qt[:, j * BLK:(j + 1) * BLK]
        return carry

    for i in range(2):
        some(i, 0)

    def emit(b, hp, top, den):
        state[b, hp, pl.ds(0, 64)] = top
        state[b, hp, pl.ds(64, 8)] = den

    attend_part(0, lists, parity[0], q, kscr, vscr, emit)


def middle_kernel(part, count, parity, lists, gain, wk, wv_t, q, state_in, *refs):
    srcs, refs = refs[:count], refs[count:]
    state, kscr, vscr, sems = refs
    came = fetch([(srcs[i], kscr.at[pl.ds(4 * i, 4)]) for i in range(count)], sems)
    clear(kscr, vscr, 4 * count)
    for copy in came:
        copy.wait()
    project_in_place(4 * count, 4, gain, wk, wv_t, kscr, vscr, 0)

    def emit(b, hp, top, den):
        state[b, hp, pl.ds(0, 64)] = state_in[b, hp, pl.ds(0, 64)] + top
        state[b, hp, pl.ds(64, 8)] = state_in[b, hp, pl.ds(64, 8)] + den

    attend_part(part, lists, parity[0], q, kscr, vscr, emit)


def last_kernel(
    parity, lists, slots, counts, gain_attn, wk, wv_t, gain_mlp,
    far_i, up, down, own_hbm, par_o, par_i, far_o, q_hbm, state_hbm, wo_hbm, w_in_hbm, w_back_hbm,
    out_hbm,
    kscr, vscr, att, hid, chk, own, q, state, wo, w_in, w_back, out, sems, out_sems,
):
    late = fetch(
        (
            (q_hbm, q), (state_hbm, state), (own_hbm, own),
            (wo_hbm, wo), (w_in_hbm, w_in), (w_back_hbm, w_back),
        ),
        sems,
    )
    clear(kscr, vscr, NULL)
    chk[...] = jnp.zeros_like(chk)
    weights = (gain_attn, wk, wv_t, kscr, vscr)
    for src, base in ((up, UP), (down, DOWN), (far_i, FAR_I)):
        project(src[...], gain_attn[...], wk[...], wv_t[...], kscr, vscr, base)
    late[0].wait()
    late[1].wait()

    def settle(b, hp, top, den):
        inv = 1.0 / den
        h0 = top[:, 0:BLK] * inv[:, 0:BLK]
        h1 = top[:, BLK:2 * BLK] * inv[:, BLK:2 * BLK]
        both = jnp.concatenate([h0, h1], axis=0).T.astype(BF16)
        att[pl.ds(pl.multiple_of(b * BLK, BLK), BLK), head_lanes(hp)] = both

    def emit(b, hp, top, den):
        top = top + state[b, hp, pl.ds(0, 64)]
        den = den[0:1] + state[b, hp, pl.ds(64, 1)]
        good = (den > 2.0 ** -60) & (den < 2.0 ** 100)
        chk[...] = jnp.maximum(chk[...], jnp.where(good, 0.0, 1.0))
        settle(b, hp, top, den)

    attend_part(3, lists, parity[0], q, kscr, vscr, emit)
    late[2].wait()

    @pl.when(jnp.max(chk[...]) > 0.5)
    def _():
        again = fetch(
            (
                (own_hbm, kscr.at[pl.ds(OWN, 8)]), (par_o, kscr.at[pl.ds(PAR_O, 4)]),
                (par_i, kscr.at[pl.ds(PAR_I, 4)]), (far_o, kscr.at[pl.ds(FAR_O, 4)]),
            ),
            out_sems,
        )
        for copy in again:
            copy.wait()
        project_in_place(SLOTS - OWN, 1, *weights, OWN)

        def pair(i, carry):
            b, hp = i // PAIRS, i % PAIRS
            qb = query_of(q, b, hp)

            def scores(n):
                return dot(kscr[slots[b, n], :, head_lanes(hp)], qb)

            def top_of(n, m):
                return jnp.maximum(m, jnp.max(scores(n), axis=0, keepdims=True))

            top = lax.fori_loop(0, counts[b], top_of, jnp.full((1, 256), -3e38, F32))

            def add(n, o):
                p = jnp.exp(scores(n) - top).astype(BF16)
                return o + dot(vscr[slots[b, n], hp], p)

            o = lax.fori_loop(0, counts[b], add, jnp.zeros((144, 256), F32))
            parts = jnp.concatenate([o[0:64, 0:BLK], o[64:BLK, BLK:2 * BLK]], axis=1)
            settle(b, hp, parts, o[BLK:BLK + 1])
            return carry

        lax.fori_loop(0, 8 * PAIRS, pair, 0)

    for copy in late[3:]:
        copy.wait()

    def leaving(i):
        blocks = pl.ds(4 * i, 4)
        return pltpu.make_async_copy(out.at[blocks], out_hbm.at[blocks], out_sems.at[i])

    def mlp(i, carry):
        rows = pl.ds(pl.multiple_of(i * 512, 512), 512)
        mid = own[pl.ds(4 * i, 4)].astype(F32).reshape(512, D) + dot(att[rows], wo[...])
        y = normalize(mid, gain_mlp[...]).astype(BF16)
        for j in range(0, FFN, 256):
            for r in range(0, 512, BLK):
                hid[r:r + BLK, j:j + 256] = gelu(dot(y[r:r + BLK], w_in[:, j:j + 256])).astype(BF16)
        for n in range(0, D, 256):
            res = mid[:, n:n + 256] + dot(hid[...], w_back[:, n:n + 256])
            out[pl.ds(4 * i, 4), :, n:n + 256] = res.astype(BF16).reshape(4, BLK, 256)
        leaving(i).start()
        return carry

    lax.fori_loop(0, 2, mlp, 0)
    for i in range(2):
        leaving(i).wait()


def shards(
    nodes, neighbours, live, gain_attn, w_query, w_key, w_value, w_out, gain_mlp, w_in, w_back
):
    rows, cols, nblk, width = nodes.shape
    blocks = rows * cols
    smem = pl.BlockSpec(memory_space=pltpu.SMEM)
    vmem = pl.BlockSpec(memory_space=pltpu.VMEM)
    hbm = pl.BlockSpec(memory_space=pltpu.HBM)
    state_shape = (blocks, PAIRS, 72, 256)
    q_shape = (blocks, width, nblk)
    dma = pltpu.SemaphoreType.DMA

    def kv_scratch(count):
        return [
            pltpu.VMEM((count, nblk, width), BF16),
            pltpu.VMEM((count, PAIRS, 144, nblk), BF16),
        ]

    def call(kernel, name, ins, outs, scratch, mib, gflop, mbytes, place=hbm):
        return pl.pallas_call(
            kernel,
            name=name,
            out_shape=[jax.ShapeDtypeStruct(s, t) for s, t in outs],
            in_specs=[i for i, _ in ins],
            out_specs=[place] * len(outs),
            scratch_shapes=scratch,
            compiler_params=pltpu.CompilerParams(vmem_limit_bytes=mib * 2**20),
            cost_estimate=pl.CostEstimate(
                flops=int(gflop * COST * 1e9), bytes_accessed=int(mbytes * 1e6), transcendentals=0
            ),
        )(*[v for _, v in ins])

    parity = (lax.axis_index("lon") % 2).astype(jnp.int32).reshape(1)
    slots = slots_of(neighbours, live, rows, cols)
    lists = [picked(slots, part) for part in range(4)]
    gain1, gain2 = gain_attn.reshape(1, width), gain_mlp.reshape(1, width)

    own = nodes.reshape(blocks, nblk, width)
    par_o = to_partner(nodes[::3].reshape(4, nblk, width))
    par_i = to_partner(own[2:6])
    far_o = along_z(par_o)
    q, state, wv_t = call(
        own_kernel, "own_part",
        [(smem, parity), (smem, lists[0]), (vmem, own), (vmem, gain1)]
        + [(vmem, w_query), (vmem, w_key), (vmem, w_value)],
        [(q_shape, BF16), (state_shape, F32), ((width, width), BF16)],
        [pltpu.VMEM((width, width), BF16)] + kv_scratch(9),
        26, 7, 6, vmem,
    )

    def middle(part, name, srcs, state, gflop):
        return call(
            lambda *refs: middle_kernel(part, len(srcs), *refs), name,
            [(smem, parity), (smem, lists[part])]
            + [(vmem, gain1), (vmem, w_key), (vmem, wv_t), (vmem, q), (vmem, state)]
            + [(hbm, s) for s in srcs],
            [(state_shape, F32)],
            kv_scratch(4 * len(srcs) + 1) + [dma((len(srcs),))],
            22, gflop, 8, vmem,
        )[0]

    state = middle(1, "outer_partner_part", [par_o], state, 3)
    state, par_i = lax.optimization_barrier((state, par_i))
    far_i = along_z(par_i)
    own_e, par_e, far_e, _ = lax.optimization_barrier((own, par_o, far_o, par_i))
    up = to_next_lat(jnp.concatenate([own_e[6:], par_e[2:], far_e[2:]], axis=0))
    down = to_last_lat(jnp.concatenate([own_e[:2], par_e[:2], far_e[:2]], axis=0))
    state = middle(2, "inner_partner_part", [par_i, far_o], state, 6)
    (result,) = call(
        last_kernel, "last_part_and_mlp",
        [(smem, parity), (smem, lists[3]), (smem, slots), (smem, live.reshape(blocks))]
        + [(vmem, gain1), (vmem, w_key), (vmem, wv_t), (vmem, gain2)]
        + [(vmem, v) for v in (far_i, up, down)] + [(hbm, v) for v in (own, par_o, par_i, far_o)]
        + [(hbm, q), (hbm, state), (hbm, w_out), (hbm, w_in), (hbm, w_back)],
        [((blocks, nblk, width), BF16)],
        kv_scratch(SLOTS) + [
            pltpu.VMEM((blocks * nblk, width), BF16),
            pltpu.VMEM((512, FFN), BF16),
            pltpu.VMEM((1, 256), F32),
            pltpu.VMEM((blocks, nblk, width), BF16),
            pltpu.VMEM(q_shape, BF16),
            pltpu.VMEM(state_shape, F32),
            pltpu.VMEM((width, width), BF16),
            pltpu.VMEM((width, FFN), BF16),
            pltpu.VMEM((FFN, width), BF16),
            pltpu.VMEM((blocks, nblk, width), BF16),
            dma((6,)),
            dma((4,)),
        ],
        36, 14, 16,
    )
    return result.reshape(rows, cols, nblk, width)


def solution(mesh):
    placed = (
        P("lat", "lon", None, None),
        P("lat", "lon", None),
        P("lat", "lon"),
        P(), P(), P(), P(), P(), P(), P(), P(),
    )
    return jax.shard_map(
        shards, mesh=mesh, in_specs=placed, out_specs=P("lat", "lon", None, None), check_vma=False
    )
```

```python
import jax
import jax.numpy as jnp
from jax import lax
from jax.experimental import pallas as pl
from jax.experimental.pallas import tpu as pltpu
from jax.sharding import PartitionSpec as P

HEADS = 8
NBR = 12
BLK = 128
D = 512
FFN = 2048
PAIRS = 4
COST = 20
AXES = ("lat", "lon")
F32 = jnp.float32
BF16 = jnp.bfloat16
NT = (((1,), (1,)), ((), ()))
FAR_I, UP, DOWN, NULL, OWN, PAR_O, PAR_I, FAR_O, SLOTS = 0, 4, 10, 16, 17, 25, 29, 33, 37
PARTS = ((OWN, PAR_O), (PAR_O, PAR_I), (PAR_I, SLOTS), (FAR_I, NULL))
LENGTHS = {
    (False, 0): (6, 2, 4, 4),
    (False, 1): (6, 2, 6, 2),
    (True, 0): (4, 2, 4, 8),
    (True, 1): (4, 2, 4, 6),
}


def moved(value, target):
    lats, lons = lax.axis_size("lat"), lax.axis_size("lon")
    pairs = []
    for la in range(lats):
        for lo in range(lons):
            to = target(la, lo)
            if to is not None:
                pairs.append((la * lons + lo, to[0] * lons + to[1]))
    return lax.ppermute(value, AXES, pairs)


def to_partner(value):
    return moved(value, lambda la, lo: (la, lo ^ 1))


def along_z(value):
    lons = lax.axis_size("lon")
    return moved(value, lambda la, lo: (la, (lo + (2 if lo % 2 == 0 else -2)) % lons))


def to_next_lat(value):
    lats = lax.axis_size("lat")
    return moved(value, lambda la, lo: (la + 1, lo) if la + 1 < lats else None)


def to_last_lat(value):
    return moved(value, lambda la, lo: (la - 1, lo) if la > 0 else None)


def slots_of(neighbours, live, rows, cols):
    total_lon = cols * lax.axis_size("lon")
    lat = lax.axis_index("lat")
    lon = lax.axis_index("lon")
    dr = neighbours // total_lon - lat * rows
    dc = (neighbours % total_lon - lon * cols + 2) % total_lon
    side = jnp.where(dc < 2, 0, 1)
    partner_side = jnp.where(lon % 2 == 0, 1, 0)
    kind = jnp.where((dc == 2) | (dc == 3), 0, jnp.where(side == partner_side, 1, 2))
    col = dc % 2
    outer = (dr == 0) | (dr == 3)
    place = jnp.where(outer, dr // 3, dr - 1) * 2 + col
    partner = jnp.where(outer, PAR_O, PAR_I) + place
    far = jnp.where(outer, FAR_O, FAR_I) + place
    inner = jnp.where(kind == 0, OWN + dr * 2 + col, jnp.where(kind == 1, partner, far))
    edge = kind * 2 + col
    slot = jnp.where(dr < 0, UP + edge, jnp.where(dr >= rows, DOWN + edge, inner))
    usable = jnp.arange(NBR, dtype=jnp.int32) < live[..., None]
    slot = jnp.where(usable, jnp.clip(slot, 0, SLOTS - 1), NULL)
    return slot.reshape(rows * cols, NBR)


def picked(slots, part):
    low, high = PARTS[part]
    width = max(n[part] for n in LENGTHS.values())
    inside = (slots >= low) & (slots < high)
    place = jnp.cumsum(inside.astype(jnp.int32), axis=-1) - 1
    spot = jnp.where(inside, place, -1)[:, :, None] == jnp.arange(width, dtype=jnp.int32)
    return (high - low) + jnp.sum(jnp.where(spot, slots[:, :, None] - high, 0), axis=1)


def normalize(x, gain):
    centre = x - jnp.mean(x, axis=-1, keepdims=True)
    spread = jnp.mean(centre * centre, axis=-1, keepdims=True)
    return centre * lax.rsqrt(spread + 1e-05) * gain


def dot(a, b):
    return jnp.dot(a, b, preferred_element_type=F32)


def gelu(x):
    half = 0.5 * x
    return half + half * jnp.tanh(x * (0.7978845608028654 + 0.035677408136300125 * (x * x)))


def project(x, gain, wk, wv_t, kscr, vscr, base):
    count = x.shape[0]
    y = normalize(x.astype(F32).reshape(count * BLK, D), gain).astype(BF16)
    k = dot(y, wk).astype(BF16)
    vt = lax.dot_general(wv_t, y, NT, preferred_element_type=F32).astype(BF16)
    for i in range(count):
        kscr[base + i] = k[i * BLK:(i + 1) * BLK]
        for hp in range(PAIRS):
            vscr[base + i, hp, pl.ds(0, BLK)] = vt[hp * BLK:(hp + 1) * BLK, i * BLK:(i + 1) * BLK]
            vscr[base + i, hp, pl.ds(BLK, 16)] = jnp.ones((16, BLK), BF16)
    return y


def clear(kscr, vscr, at):
    kscr[at] = jnp.zeros((BLK, D), BF16)
    vscr[at] = jnp.zeros((PAIRS, 144, BLK), BF16)


def head_lanes(hp):
    return pl.ds(hp * BLK if isinstance(hp, int) else pl.multiple_of(hp * BLK, BLK), BLK)


def query_of(q, b, hp):
    zeros = jnp.zeros((64, BLK), BF16)
    h0 = q[b, pl.ds(hp * BLK, 64)]
    h1 = q[b, pl.ds(hp * BLK + 64, 64)]
    return jnp.concatenate(
        [jnp.concatenate([h0, zeros], axis=1), jnp.concatenate([zeros, h1], axis=1)], axis=0
    )


def attend(items, q, kscr, vscr, emit):
    work = [(b, hp, ids) for b, ids in items for hp in range(PAIRS)]
    before = None
    for item in work + [None]:
        probs = None
        if item is not None:
            b, hp, ids = item
            qb = query_of(q, b, hp)
            probs = [
                jnp.exp(dot(kscr[i, :, hp * BLK:(hp + 1) * BLK], qb)).astype(BF16) for i in ids
            ]
        if before is not None:
            (b0, hp0, ids0), probs0 = before
            vals = jnp.concatenate([vscr[i, hp0] for i in ids0], axis=1)
            o = dot(vals, jnp.concatenate(probs0, axis=0))
            top = jnp.concatenate([o[0:64, 0:BLK], o[64:BLK, BLK:2 * BLK]], axis=1)
            emit(b0, hp0, top, o[BLK:BLK + 8])
        before = (item, probs)


def attend_part(part, lists, parity, q, kscr, vscr, emit):
    groups = {}
    for (edge, side), lengths in LENGTHS.items():
        groups.setdefault(lengths[part], []).append((int(edge), side))
    for n, members in groups.items():
        at_once = 1 if part == 2 else 2

        def some(j, carry, n=n, members=members, at_once=at_once):
            items = []
            for e in range(at_once):
                i = j * at_once + e
                member, second = i // 2, i % 2
                edge, side = members[0]
                for m in range(1, len(members)):
                    edge = jnp.where(member == m, members[m][0], edge)
                    side = jnp.where(member == m, members[m][1], side)
                row = edge * 3 * second + (1 - edge) * (1 + second)
                b = row * 2 + jnp.bitwise_xor(parity, side)
                items.append((b, [lists[b, t] for t in range(n)]))
            attend(items, q, kscr, vscr, emit)
            return carry

        lax.fori_loop(0, 2 * len(members) // at_once, some, 0)


def fetch(pairs, sems):
    copies = [pltpu.make_async_copy(src, dst, sems.at[i]) for i, (src, dst) in enumerate(pairs)]
    for copy in copies:
        copy.start()
    return copies


def project_in_place(count, per, gain, wk, wv_t, kscr, vscr, base):
    def some(i, carry):
        at = base + per * i
        project(kscr[pl.ds(at, per)], gain[...], wk[...], wv_t[...], kscr, vscr, at)
        return carry

    lax.fori_loop(0, count // per, some, 0)


def own_kernel(
    parity, lists, own, gain, wq, wk, wv, q, state, wv_t,
    wq_t, kscr, vscr,
):
    clear(kscr, vscr, 8)
    wq_t[...] = wq[...].T
    wv_t[...] = wv[...].T

    def some(i, carry):
        y = project(own[pl.ds(4 * i, 4)], gain[...], wk[...], wv_t[...], kscr, vscr, 4 * i)
        qt = lax.dot_general(wq_t[...], y, NT, preferred_element_type=F32).astype(BF16)
        qt = qt * jnp.asarray(0.125, BF16)
        for j in range(4):
            q[4 * i + j] = qt[:, j * BLK:(j + 1) * BLK]
        return carry

    for i in range(2):
        some(i, 0)

    def emit(b, hp, top, den):
        state[b, hp, pl.ds(0, 64)] = top
        state[b, hp, pl.ds(64, 8)] = den

    attend_part(0, lists, parity[0], q, kscr, vscr, emit)


def middle_kernel(part, count, parity, lists, gain, wk, wv_t, q, state_in, *refs):
    srcs, refs = refs[:count], refs[count:]
    state, kscr, vscr, sems = refs
    came = fetch([(srcs[i], kscr.at[pl.ds(4 * i, 4)]) for i in range(count)], sems)
    clear(kscr, vscr, 4 * count)
    for copy in came:
        copy.wait()
    project_in_place(4 * count, 4, gain, wk, wv_t, kscr, vscr, 0)

    def emit(b, hp, top, den):
        state[b, hp, pl.ds(0, 64)] = state_in[b, hp, pl.ds(0, 64)] + top
        state[b, hp, pl.ds(64, 8)] = state_in[b, hp, pl.ds(64, 8)] + den

    attend_part(part, lists, parity[0], q, kscr, vscr, emit)


def last_kernel(
    parity, lists, slots, counts, gain_attn, wk, wv_t, gain_mlp,
    far_i, up, down, own, q, state, wo, w_in, w_back, par_o, par_i, far_o,
    out_hbm,
    kscr, vscr, att, hid, chk, out, out_sems,
):
    clear(kscr, vscr, NULL)
    chk[...] = jnp.zeros_like(chk)
    weights = (gain_attn, wk, wv_t, kscr, vscr)
    for src, base in ((up, UP), (down, DOWN), (far_i, FAR_I)):
        project(src[...], gain_attn[...], wk[...], wv_t[...], kscr, vscr, base)

    def settle(b, hp, top, den):
        inv = 1.0 / den
        h0 = top[:, 0:BLK] * inv[:, 0:BLK]
        h1 = top[:, BLK:2 * BLK] * inv[:, BLK:2 * BLK]
        both = jnp.concatenate([h0, h1], axis=0).T.astype(BF16)
        att[pl.ds(pl.multiple_of(b * BLK, BLK), BLK), head_lanes(hp)] = both

    def emit(b, hp, top, den):
        top = top + state[b, hp, pl.ds(0, 64)]
        den = den[0:1] + state[b, hp, pl.ds(64, 1)]
        good = (den > 2.0 ** -60) & (den < 2.0 ** 100)
        chk[...] = jnp.maximum(chk[...], jnp.where(good, 0.0, 1.0))
        settle(b, hp, top, den)

    attend_part(3, lists, parity[0], q, kscr, vscr, emit)

    @pl.when(jnp.max(chk[...]) > 0.5)
    def _():
        again = fetch(
            (
                (own, kscr.at[pl.ds(OWN, 8)]), (par_o, kscr.at[pl.ds(PAR_O, 4)]),
                (par_i, kscr.at[pl.ds(PAR_I, 4)]), (far_o, kscr.at[pl.ds(FAR_O, 4)]),
            ),
            out_sems,
        )
        for copy in again:
            copy.wait()
        project_in_place(SLOTS - OWN, 1, *weights, OWN)

        def pair(i, carry):
            b, hp = i // PAIRS, i % PAIRS
            qb = query_of(q, b, hp)

            def scores(n):
                return dot(kscr[slots[b, n], :, head_lanes(hp)], qb)

            def top_of(n, m):
                return jnp.maximum(m, jnp.max(scores(n), axis=0, keepdims=True))

            top = lax.fori_loop(0, counts[b], top_of, jnp.full((1, 256), -3e38, F32))

            def add(n, o):
                p = jnp.exp(scores(n) - top).astype(BF16)
                return o + dot(vscr[slots[b, n], hp], p)

            o = lax.fori_loop(0, counts[b], add, jnp.zeros((144, 256), F32))
            parts = jnp.concatenate([o[0:64, 0:BLK], o[64:BLK, BLK:2 * BLK]], axis=1)
            settle(b, hp, parts, o[BLK:BLK + 1])
            return carry

        lax.fori_loop(0, 8 * PAIRS, pair, 0)

    def leaving(i):
        blocks = pl.ds(4 * i, 4)
        return pltpu.make_async_copy(out.at[blocks], out_hbm.at[blocks], out_sems.at[i])

    def mlp(i, carry):
        rows = pl.ds(pl.multiple_of(i * 512, 512), 512)
        mid = own[pl.ds(4 * i, 4)].astype(F32).reshape(512, D) + dot(att[rows], wo[...])
        y = normalize(mid, gain_mlp[...]).astype(BF16)
        for j in range(0, FFN, 256):
            for r in range(0, 512, BLK):
                hid[r:r + BLK, j:j + 256] = gelu(dot(y[r:r + BLK], w_in[:, j:j + 256])).astype(BF16)
        for n in range(0, D, 256):
            res = mid[:, n:n + 256] + dot(hid[...], w_back[:, n:n + 256])
            out[pl.ds(4 * i, 4), :, n:n + 256] = res.astype(BF16).reshape(4, BLK, 256)
        leaving(i).start()
        return carry

    lax.fori_loop(0, 2, mlp, 0)
    for i in range(2):
        leaving(i).wait()


def shards(
    nodes, neighbours, live, gain_attn, w_query, w_key, w_value, w_out, gain_mlp, w_in, w_back
):
    rows, cols, nblk, width = nodes.shape
    blocks = rows * cols
    smem = pl.BlockSpec(memory_space=pltpu.SMEM)
    vmem = pl.BlockSpec(memory_space=pltpu.VMEM)
    hbm = pl.BlockSpec(memory_space=pltpu.HBM)
    state_shape = (blocks, PAIRS, 72, 256)
    q_shape = (blocks, width, nblk)
    dma = pltpu.SemaphoreType.DMA

    def kv_scratch(count):
        return [
            pltpu.VMEM((count, nblk, width), BF16),
            pltpu.VMEM((count, PAIRS, 144, nblk), BF16),
        ]

    def call(kernel, name, ins, outs, scratch, mib, gflop, mbytes, place=hbm):
        return pl.pallas_call(
            kernel,
            name=name,
            out_shape=[jax.ShapeDtypeStruct(s, t) for s, t in outs],
            in_specs=[i for i, _ in ins],
            out_specs=[place] * len(outs),
            scratch_shapes=scratch,
            compiler_params=pltpu.CompilerParams(vmem_limit_bytes=mib * 2**20),
            cost_estimate=pl.CostEstimate(
                flops=int(gflop * COST * 1e9), bytes_accessed=int(mbytes * 1e6), transcendentals=0
            ),
        )(*[v for _, v in ins])

    parity = (lax.axis_index("lon") % 2).astype(jnp.int32).reshape(1)
    slots = slots_of(neighbours, live, rows, cols)
    lists = [picked(slots, part) for part in range(4)]
    gain1, gain2 = gain_attn.reshape(1, width), gain_mlp.reshape(1, width)

    own = nodes.reshape(blocks, nblk, width)
    par_o = to_partner(nodes[::3].reshape(4, nblk, width))
    par_i = to_partner(own[2:6])
    far_o = along_z(par_o)
    q, state, wv_t = call(
        own_kernel, "own_part",
        [(smem, parity), (smem, lists[0]), (vmem, own), (vmem, gain1)]
        + [(vmem, w_query), (vmem, w_key), (vmem, w_value)],
        [(q_shape, BF16), (state_shape, F32), ((width, width), BF16)],
        [pltpu.VMEM((width, width), BF16)] + kv_scratch(9),
        26, 7, 6, vmem,
    )

    def middle(part, name, srcs, state, gflop):
        return call(
            lambda *refs: middle_kernel(part, len(srcs), *refs), name,
            [(smem, parity), (smem, lists[part])]
            + [(vmem, gain1), (vmem, w_key), (vmem, wv_t), (vmem, q), (vmem, state)]
            + [(hbm, s) for s in srcs],
            [(state_shape, F32)],
            kv_scratch(4 * len(srcs) + 1) + [dma((len(srcs),))],
            22, gflop, 8, vmem,
        )[0]

    state = middle(1, "outer_partner_part", [par_o], state, 3)
    state, par_i = lax.optimization_barrier((state, par_i))
    far_i = along_z(par_i)
    own_e, par_e, far_e, _ = lax.optimization_barrier((own, par_o, far_o, par_i))
    up = to_next_lat(jnp.concatenate([own_e[6:], par_e[2:], far_e[2:]], axis=0))
    down = to_last_lat(jnp.concatenate([own_e[:2], par_e[:2], far_e[:2]], axis=0))
    state = middle(2, "inner_partner_part", [par_i, far_o], state, 6)
    (result,) = call(
        last_kernel, "last_part_and_mlp",
        [(smem, parity), (smem, lists[3]), (smem, slots), (smem, live.reshape(blocks))]
        + [(vmem, gain1), (vmem, w_key), (vmem, wv_t), (vmem, gain2)]
        + [(vmem, v) for v in (far_i, up, down, own, q, state, w_out, w_in, w_back)]
        + [(hbm, v) for v in (par_o, par_i, far_o)],
        [((blocks, nblk, width), BF16)],
        kv_scratch(SLOTS) + [
            pltpu.VMEM((blocks * nblk, width), BF16),
            pltpu.VMEM((512, FFN), BF16),
            pltpu.VMEM((1, 256), F32),
            pltpu.VMEM((blocks, nblk, width), BF16),
            dma((4,)),
        ],
        28, 14, 16,
    )
    return result.reshape(rows, cols, nblk, width)


def solution(mesh):
    placed = (
        P("lat", "lon", None, None),
        P("lat", "lon", None),
        P("lat", "lon"),
        P(), P(), P(), P(), P(), P(), P(), P(),
    )
    return jax.shard_map(
        shards, mesh=mesh, in_specs=placed, out_specs=P("lat", "lon", None, None), check_vma=False
    )
```
